32 devices in a mesh: gx: 16 (over z, x, core), gy: 2 (over y).
Axes of the slice: x: 2, y: 2, z: 4, core: 2. Of those that a mesh axis runs over, the one named last changes fastest.
Arguments:
- positions: float32 [3, 16, 4, 12, 128], P(None, 'gx', 'gy'), may hold values from 0 to 1
- velocities: float32 [3, 16, 4, 12, 128], P(None, 'gx', 'gy'), may hold values from -8 to 8
- counts: int32 [16, 4, 12], P('gx', 'gy'), may hold values from 64 to 128
Outputs:
- positions_out: float32 [3, 16, 4, 12, 128], P(None, 'gx', 'gy')
- velocities_out: float32 [3, 16, 4, 12, 128], P(None, 'gx', 'gy')
- forces_out: float32 [3, 16, 4, 12, 128], P(None, 'gx', 'gy')
The draws below stay inside these ranges and needn't reach their ends.
Inputs may be any that keep to these rules, and one draw needn't show every extreme that they name: `counts`: the number of atoms in a cell; slots from that number up to 128 are empty.
All inputs are finite; a program needn't handle non-finite values.
Results may differ from the reference program's by a relative error of at most 0.0001.
Values sent between devices are 32-bit elements; how exact they have to be, the bound alone decides.
A program may use at most 64 MiB of HBM per device.

```python
import jax
import jax.numpy as jnp
from jax import lax

SLOTS = 128
NCZ = 12
STEPS = 2
NCX = 16
NCY = 4


def plant(values, stream_key, smallest, high):
    dims = values.shape
    spot = [jax.random.randint(jax.random.fold_in(stream_key, axis), (), 0, dims[axis]) for axis in range(len(dims))]
    values = values.at[tuple(spot)].set(smallest)
    longest = dims.index(max(dims))
    spot[longest] = (spot[longest] + 1) % dims[longest]
    return values.at[tuple(spot)].set(high)


def level_of(own_key, extent, pieces, least, high):
    factor_of, own = 1.0, jax.random.fold_in(own_key, 6)
    for position, blocks in pieces:
        draws = jnp.exp(jax.random.uniform(jax.random.fold_in(own, position), (blocks,), jnp.float32, least / len(pieces), high / len(pieces)))
        factor_of = factor_of * jnp.repeat(draws, extent[position] // blocks).reshape([-1 if axis == position else 1 for axis in range(len(extent))])
    return factor_of


def setup_inputs(seed: int = 0) -> dict:
    key_of = jax.random.split(jax.random.key(seed), 4)
    return {
        "positions": jnp.clip(1.0 * jax.random.uniform(key_of[0], (3, NCX, NCY, NCZ, SLOTS), jnp.float32) ** level_of(key_of[0], (3, NCX, NCY, NCZ, SLOTS), ((1, 16), (2, 2)), -0.2, 0.2), 0.0, 1.0),
        "velocities": jnp.clip(jax.random.uniform(key_of[1], (3, NCX, NCY, NCZ, SLOTS), jnp.float32, -8.0, 8.0) * level_of(key_of[1], (3, NCX, NCY, NCZ, SLOTS), ((1, 16), (2, 2)), -0.4, 0.0), -8.0, 8.0),
        "counts": plant(jax.random.randint(key_of[2], (NCX, NCY, NCZ), SLOTS // 2, SLOTS + 1), jax.random.fold_in(key_of[2], 1), SLOTS // 2, SLOTS).astype(jnp.int32),
    }


TIME_STEP = 0.05
DENSITY_SCALE = 0.0625
PAIR_SCALE = 0.0625

def neighbour_block(extended, offset_id):
    start = (jnp.int32(0), offset_id // 9, offset_id // 3 % 3, offset_id % 3, jnp.int32(0))
    target = (extended.shape[0], extended.shape[1] - 2, extended.shape[2] - 2, extended.shape[3] - 2, extended.shape[4])
    return lax.dynamic_slice(extended, start, target)

def separation(center, neighbours, offset_id):
    shifts = (offset_id // 9 - 1, offset_id // 3 % 3 - 1, offset_id % 3 - 1)
    parts = []
    for component in range(3):
        moved = neighbours[component] + shifts[component].astype(center.dtype)
        parts.append(moved[..., None, :] - center[component][..., :, None])
    return parts

def pair_terms(center, extended, filled, offset_id):
    slots = center.shape[-1]
    identity = jnp.eye(slots, dtype=center.dtype)
    neighbours = neighbour_block(extended, offset_id)
    present = neighbour_block(filled, offset_id)[0]
    parts = separation(center, neighbours, offset_id)
    square = parts[0] * parts[0] + parts[1] * parts[1] + parts[2] * parts[2]
    reach = jnp.maximum(1.0 - square, 0.0)
    selfish = (offset_id == 13).astype(center.dtype) * identity
    weights_mask = present[..., None, :] * (1.0 - selfish)
    return (parts, reach, weights_mask)

def density_pass(center, extended, filled):

    def offset_step(offset_id, running):
        offset_id = offset_id.astype(jnp.int32)
        parts, reach, weights_mask = pair_terms(center, extended, filled, offset_id)
        return running + lax.optimization_barrier(jnp.sum(weights_mask * reach * reach, axis=-1))
    start_value = jnp.zeros(center.shape[1:], center.dtype)
    return DENSITY_SCALE * lax.fori_loop(0, 27, offset_step, start_value)

def force_pass(center, present_own, slope_own, extended, filled, slope_ext):

    def offset_step(offset_id, running):
        offset_id = offset_id.astype(jnp.int32)
        parts, reach, weights_mask = pair_terms(center, extended, filled, offset_id)
        slope_near = neighbour_block(slope_ext, offset_id)[0]
        both = slope_own[..., :, None] + slope_near[..., None, :]
        coupling = weights_mask * reach * (-2.0 * DENSITY_SCALE * both - 4.0 * PAIR_SCALE * reach * reach)
        return running + 2.0 * jnp.stack([lax.optimization_barrier(jnp.sum(coupling * parts[component], axis=-1)) for component in range(3)])
    start_value = jnp.zeros(center.shape, center.dtype)
    return lax.fori_loop(0, 27, offset_step, start_value) * present_own[None]

def slots_filled(amount, slots):
    places = lax.broadcasted_iota(amount.dtype, amount.shape + (slots,), amount.ndim)
    return (places < amount[..., None]).astype(amount.dtype)

def wrap_all(field):
    return jnp.pad(field, ((0, 0), (1, 1), (1, 1), (1, 1), (0, 0)), mode='wrap')

def forces_of(positions, amount):
    slots = positions.shape[-1]
    filled_own = slots_filled(amount, slots)
    extended = wrap_all(positions)
    filled = wrap_all(filled_own[None])

    def row_density(row_index):
        center = lax.dynamic_slice_in_dim(positions, row_index, 1, 1)
        near = lax.dynamic_slice_in_dim(extended, row_index, 3, 1)
        near_filled = lax.dynamic_slice_in_dim(filled, row_index, 3, 1)
        return density_pass(center, near, near_filled)[0]
    rows = jnp.arange(NCX, dtype=jnp.int32)
    density = lax.map(row_density, rows)
    slope = -0.5 / jnp.sqrt(1.0 + density)
    slope_ext = wrap_all(slope[None])

    def row_force(row_index):
        center = lax.dynamic_slice_in_dim(positions, row_index, 1, 1)
        near = lax.dynamic_slice_in_dim(extended, row_index, 3, 1)
        near_filled = lax.dynamic_slice_in_dim(filled, row_index, 3, 1)
        present_own = lax.dynamic_slice_in_dim(filled_own, row_index, 1, 0)
        slope_own = lax.dynamic_slice_in_dim(slope, row_index, 1, 0)
        near_slope = lax.dynamic_slice_in_dim(slope_ext, row_index, 3, 1)
        return force_pass(center, present_own, slope_own, near, near_filled, near_slope)[:, 0]
    return jnp.moveaxis(lax.map(row_force, rows), 0, 1)

def reference(positions, velocities, counts):
    amount = counts.astype(jnp.float32)
    pushed = forces_of(positions, amount)
    for step_index in range(STEPS):
        velocities = velocities + 0.5 * TIME_STEP * pushed
        positions = positions + TIME_STEP * velocities
        pushed = forces_of(positions, amount)
        velocities = velocities + 0.5 * TIME_STEP * pushed
    return (positions, velocities, pushed)
```

```python
import functools

import jax
import jax.numpy as jnp
from jax import lax
from jax.experimental import pallas as pl
from jax.experimental.pallas import tpu as pltpu
from jax.sharding import PartitionSpec as P

STEPS = 2
TIME_STEP = 0.05
DENSITY_SCALE = 0.0625
PAIR_SCALE = 0.0625
ABSENT = 1.0e6

FEATURES = 32
ROWS = 16
NEAR = (-1, 0, 1)
MESH = pl.DeviceIdType.MESH


def split3(value):
    high = value.astype(jnp.bfloat16).astype(jnp.float32)
    rest = value - high
    middle = rest.astype(jnp.bfloat16).astype(jnp.float32)
    return high, middle, rest - middle


def split2(value):
    high = value.astype(jnp.bfloat16).astype(jnp.float32)
    return high, value - high


def directions():
    return [(dx, dy) for dx in NEAR for dy in NEAR if (dx, dy) != (0, 0)]


def neighbour(sizes, dx, dy):
    gx = lax.rem(lax.axis_index("gx") + sizes[0] + dx, sizes[0])
    gy = lax.rem(lax.axis_index("gy") + sizes[1] + dy, sizes[1])
    return (gx, gy)


def exchange(buffer, sizes, columns, send_sem, recv_sem):
    copies = []
    for slot, (dx, dy) in enumerate(directions()):
        first, count, landing = 1, columns, 1
        if dy == 1:
            first, count, landing = columns, 1, 0
        if dy == -1:
            first, count, landing = 1, 1, columns + 1
        copies.append(
            pltpu.make_async_remote_copy(
                src_ref=buffer.at[1, pl.ds(first, count)],
                dst_ref=buffer.at[1 - dx, pl.ds(landing, count)],
                send_sem=send_sem.at[slot],
                recv_sem=recv_sem.at[slot],
                device_id=neighbour(sizes, dx, dy),
                device_id_type=MESH,
            )
        )
    for copy in copies:
        copy.start()
    return copies


def kernel(
    sizes, columns, depth, slots,
    pos_in, vel_in, mask_in, pos_out, vel_out, force_out,
    places, slopes, frame, own_rows, near_rows, near_cols, self_rows, blocks,
    sum_rows, sums, slope_rows, slope_sums, held, cubes, partial,
    place_send, place_recv, slope_send, slope_recv,
):
    wide = columns + 2
    f32, bf16 = jnp.float32, jnp.bfloat16
    cells = columns * depth

    barrier = pltpu.get_barrier_semaphore()
    greeted = [(dx, dy) for dx, dy in directions() if not (sizes[1] == 2 and dy == -1)]
    for dx, dy in greeted:
        pl.semaphore_signal(barrier, inc=1, device_id=neighbour(sizes, dx, dy), device_id_type=MESH)
    pl.semaphore_wait(barrier, len(greeted))

    for component in range(3):
        for column in range(columns):
            places[1, 1 + column, component] = pos_in[component, column]
            vel_out[component, column] = vel_in[component, column]
    for column in range(columns):
        places[1, 1 + column, 3] = mask_in[column]

    near_rows[...] = jnp.zeros_like(near_rows)
    self_rows[...] = jnp.zeros_like(self_rows)
    blocks[...] = jnp.zeros_like(blocks)
    sum_rows[...] = jnp.zeros_like(sum_rows)
    slope_rows[...] = jnp.zeros_like(slope_rows)
    own_rows[...] = jnp.zeros_like(own_rows)
    ones = jnp.ones((depth, slots), f32)

    def put(ref, index, row, stride, value):
        ref[index + (pl.ds(row, depth, stride=stride), slice(None))] = value

    for v in range(wide):
        for u in range(3):
            for row in (21, 22, 23):
                put(near_rows, (v,), u * FEATURES + row, 128, ones)
            put(sum_rows, (u, v), 3, ROWS, ones)
            put(sum_rows, (u, v), 14, ROWS, ones)
    for column in range(columns):
        put(own_rows, (column,), 3, 8, ones)
        for r in range(3):
            for row in (18, 19, 20):
                put(self_rows, (r, column), row, FEATURES, ones)

    def build_column(u, v):
        mask = places[u, v, 3]
        spots = (
            places[u, v, 0] + (u - 1.5),
            places[u, v, 1] + (v - 1.0 - 0.5 * columns),
            places[u, v, 2] - 0.5,
        )
        norm = jnp.where(mask > 0.0, spots[0] * spots[0] + spots[1] * spots[1] + spots[2] * spots[2], ABSENT)
        base = u * FEATURES
        for c in range(3):
            frame[u, v, c] = spots[c]
            h, m, l = split3(spots[c])
            for place, value in enumerate((h, h, m, h, l, m)):
                put(near_rows, (v,), base + 6 * c + place, 128, value)
            put(sum_rows, (u, v), c, ROWS, h)
            put(sum_rows, (u, v), 4 + c, ROWS, m)
            put(sum_rows, (u, v), 8 + c, ROWS, l)
        for place, value in enumerate(split3(-norm)):
            put(near_rows, (v,), base + 18 + place, 128, value)

    def build_own(column):
        v = column + 1
        spots = (
            places[1, v, 0] - 0.5,
            places[1, v, 1] + (v - 1.0 - 0.5 * columns),
            places[1, v, 2] - 0.5,
        )
        for c in range(3):
            put(own_rows, (column,), c, 8, spots[c])
        for r in range(3):
            moved = (spots[0], spots[1], spots[2] - (r - 1.0))
            norm = moved[0] * moved[0] + moved[1] * moved[1] + moved[2] * moved[2]
            for c in range(3):
                h, m, l = split3(2.0 * moved[c])
                for place, value in enumerate((h, m, h, l, h, m)):
                    put(self_rows, (r, column), 6 * c + place, FEATURES, value)
            for place, value in enumerate(split3(1.0 - norm)):
                put(self_rows, (r, column), 21 + place, FEATURES, value)

    def build_slopes(u, v):
        near = slopes[u, v]
        for c in range(3):
            h, m = split2(near * frame[u, v, c])
            put(slope_rows, (u, v), c, ROWS, h)
            put(slope_rows, (u, v), 4 + c, ROWS, m)
        h, m = split2(near)
        put(slope_rows, (u, v), 3, ROWS, h)
        put(slope_rows, (u, v), 7, ROWS, m)
        put(slope_rows, (u, v), 10, ROWS, h)
        put(slope_rows, (u, v), 14, ROWS, m)

    row_ids = lax.broadcasted_iota(jnp.int32, (ROWS, slots), 0)

    def scaled(first):
        return [jnp.where(row_ids >= first, float(r), 1.0).astype(bf16) for r in NEAR]

    def rows_of(ref, u, column, layers, scales):
        parts = []
        for q in range(3):
            for r in range(3):
                start = pl.multiple_of(layers[r] * ROWS, ROWS)
                parts.append(ref[u, column + q, pl.ds(start, ROWS), :] * scales[r])
        return jnp.concatenate(parts, axis=1)

    def folded(total):
        both = total[:, :slots] + total[:, slots:]
        half = both[:8] + both[8:]
        return half[:4] + half[4:]

    def spread(total, own):
        return total - own[:4] * total[3:4]

    def layers_of(z):
        return [lax.rem(z + r + depth, depth) for r in NEAR]

    def first_pass(cell, carry):
        column, z = lax.div(cell, depth), lax.rem(cell, depth)
        layers = layers_of(z)
        for r in range(3):
            start = pl.multiple_of(z * FEATURES, FEATURES)
            block = self_rows[r, column, pl.ds(start, FEATURES), :].astype(bf16)
            for u in range(3):
                blocks[r, pl.ds(u * FEATURES, FEATURES), pl.ds(u * slots, slots)] = block
        density = jnp.zeros((8, slots), f32)
        for q in range(3):
            for r in range(3):
                start = pl.multiple_of(layers[r] * 128, 128)
                near = near_cols[column + q, pl.ds(start, slots), :]
                for u in range(3):
                    reach = jnp.dot(near, blocks[r, :, u * slots:(u + 1) * slots], preferred_element_type=f32)
                    reach = jnp.maximum(reach, 0.0)
                    square = reach * reach
                    density = density + jnp.sum(square.reshape(slots // 8, 8, slots), axis=0)
                    cube = square * reach
                    high = reach.astype(bf16)
                    low = (reach - high.astype(f32)).astype(bf16)
                    rows = pl.ds((q * 3 + r) * slots, slots)
                    held[cell * 3 + u, rows, pl.ds(0, slots)] = high
                    held[cell * 3 + u, rows, pl.ds(slots, slots)] = low
                    high = cube.astype(bf16)
                    low = (cube - high.astype(f32)).astype(bf16)
                    cubes[u, rows, pl.ds(0, slots)] = high
                    cubes[u, rows, pl.ds(slots, slots)] = low
        own = own_rows[column, pl.ds(pl.multiple_of(z * 8, 8), 8), :]
        present = places[1, column + 1, 3, pl.ds(z, 1), :]
        density = DENSITY_SCALE * (jnp.sum(density, axis=0, keepdims=True) - present)
        slope = 2.0 * DENSITY_SCALE * 2.0 * 0.5 / jnp.sqrt(1.0 + density)
        slopes[1, column + 1, pl.ds(z, 1), :] = slope
        scales = scaled(12)
        linear = jnp.zeros((ROWS, 2 * slots), f32)
        cubic = jnp.zeros((ROWS, 2 * slots), f32)
        for u in range(3):
            lhs = rows_of(sums, u, column, layers, scales)
            linear = linear + jnp.dot(lhs, held[cell * 3 + u], preferred_element_type=f32)
            cubic = cubic + jnp.dot(lhs, cubes[u], preferred_element_type=f32)
        force = slope * spread(folded(linear), own) - (8.0 * PAIR_SCALE) * spread(folded(cubic), own)
        partial[column, pl.ds(pl.multiple_of(z * 8, 8), 4), :] = force
        return carry

    def second_pass(cell, carry):
        column, z = lax.div(cell, depth), lax.rem(cell, depth)
        layers = layers_of(z)
        own = own_rows[column, pl.ds(pl.multiple_of(z * 8, 8), 8), :]
        scales = scaled(8)
        total = jnp.zeros((ROWS, 2 * slots), f32)
        for u in range(3):
            lhs = rows_of(slope_sums, u, column, layers, scales)
            total = total + jnp.dot(lhs, held[cell * 3 + u], preferred_element_type=f32)
        where = pl.ds(pl.multiple_of(z * 8, 8), 4)
        partial[column, where, :] = partial[column, where, :] + spread(folded(total), own)
        return carry

    def turned(index, carry):
        v, z = lax.div(index, depth), lax.rem(index, depth)
        rows = pl.ds(pl.multiple_of(z * 128, 128), 128)
        near_cols[v, rows, :] = near_rows[v, rows, :].T.astype(bf16)
        return carry

    def evaluate(step, carry):
        copies = exchange(places, sizes, columns, place_send, place_recv)
        for column in range(columns):
            build_own(column)
            build_column(1, column + 1)
        for copy in copies:
            copy.wait()
        for u in range(3):
            for v in range(wide):
                if u != 1 or v in (0, wide - 1):
                    build_column(u, v)
        for u in range(3):
            for v in range(wide):
                sums[u, v] = sum_rows[u, v].astype(bf16)
        lax.fori_loop(0, wide * depth, turned, 0)
        lax.fori_loop(0, cells, first_pass, 0)
        copies = exchange(slopes, sizes, columns, slope_send, slope_recv)
        for copy in copies:
            copy.wait()
        for u in range(3):
            for v in range(wide):
                build_slopes(u, v)
                slope_sums[u, v] = slope_rows[u, v].astype(bf16)
        lax.fori_loop(0, cells, second_pass, 0)
        begin = jnp.where(step > 0, 0.5 * TIME_STEP, 0.0)
        end = jnp.where(step < STEPS, 0.5 * TIME_STEP, 0.0)
        drift = jnp.where(step < STEPS, TIME_STEP, 0.0)
        for column in range(columns):
            for c in range(3):
                force = partial[column, pl.ds(c, depth, stride=8), :] * places[1, column + 1, 3]
                force_out[c, column] = force
                speed = (vel_out[c, column] + begin * force) + end * force
                vel_out[c, column] = speed
                places[1, column + 1, c] = places[1, column + 1, c] + drift * speed
        return carry

    lax.fori_loop(0, STEPS + 1, evaluate, 0)
    for c in range(3):
        for column in range(columns):
            pos_out[c, column] = places[1, column + 1, c]


def shards(sizes, positions, velocities, counts):
    _, _, columns, depth, slots = positions.shape
    filled = lax.broadcasted_iota(jnp.int32, (columns, depth, slots), 2) < counts.reshape(columns, depth, 1)
    shape = (3, columns, depth, slots)
    wide = columns + 2
    cells = columns * depth
    f32, bf16 = jnp.float32, jnp.bfloat16
    vmem = pl.BlockSpec(memory_space=pltpu.VMEM)
    outs = pl.pallas_call(
        functools.partial(kernel, sizes, columns, depth, slots),
        out_shape=[jax.ShapeDtypeStruct(shape, f32)] * 3,
        in_specs=[vmem] * 3,
        out_specs=[vmem] * 3,
        scratch_shapes=[
            pltpu.VMEM((3, wide, 4, depth, slots), f32),
            pltpu.VMEM((3, wide, depth, slots), f32),
            pltpu.VMEM((3, wide, 3, depth, slots), f32),
            pltpu.VMEM((columns, depth * 8, slots), f32),
            pltpu.VMEM((wide, depth * 128, slots), f32),
            pltpu.VMEM((wide, depth * slots, 128), bf16),
            pltpu.VMEM((3, columns, depth * FEATURES, slots), f32),
            pltpu.VMEM((3, 128, 3 * slots), bf16),
            pltpu.VMEM((3, wide, depth * ROWS, slots), f32),
            pltpu.VMEM((3, wide, depth * ROWS, slots), bf16),
            pltpu.VMEM((3, wide, depth * ROWS, slots), f32),
            pltpu.VMEM((3, wide, depth * ROWS, slots), bf16),
            pltpu.VMEM((cells * 3, 9 * slots, 2 * slots), bf16),
            pltpu.VMEM((3, 9 * slots, 2 * slots), bf16),
            pltpu.VMEM((columns, depth * 8, slots), f32),
            pltpu.SemaphoreType.DMA((8,)),
            pltpu.SemaphoreType.DMA((8,)),
            pltpu.SemaphoreType.DMA((8,)),
            pltpu.SemaphoreType.DMA((8,)),
        ],
        compiler_params=pltpu.CompilerParams(
            collective_id=0, has_side_effects=True, vmem_limit_bytes=60 * 1024 * 1024
        ),
        name="verlet",
    )(positions.reshape(shape), velocities.reshape(shape), filled.astype(f32))
    return tuple(out.reshape(positions.shape) for out in outs)


def solution(mesh):
    grid = P(None, "gx", "gy", None, None)
    sizes = (mesh.shape["gx"], mesh.shape["gy"])
    return jax.shard_map(
        functools.partial(shards, sizes),
        mesh=mesh,
        in_specs=(grid, grid, P("gx", "gy", None)),
        out_specs=(grid, grid, grid),
        check_vma=False,
    )
```

```python
import functools

import jax
import jax.numpy as jnp
from jax import lax
from jax.experimental import pallas as pl
from jax.experimental.pallas import tpu as pltpu
from jax.sharding import PartitionSpec as P

STEPS = 2
TIME_STEP = 0.05
DENSITY_SCALE = 0.0625
PAIR_SCALE = 0.0625
ABSENT = 1.0e6

FEATURES = 32
TALL = 32
NEAR = (-1, 0, 1)
MESH = pl.DeviceIdType.MESH


def split3(value):
    high = value.astype(jnp.bfloat16).astype(jnp.float32)
    rest = value - high
    middle = rest.astype(jnp.bfloat16).astype(jnp.float32)
    return high, middle, rest - middle


def directions():
    return [(dx, dy) for dx in NEAR for dy in NEAR if (dx, dy) != (0, 0)]


def neighbour(sizes, dx, dy):
    gx = lax.rem(lax.axis_index("gx") + sizes[0] + dx, sizes[0])
    gy = lax.rem(lax.axis_index("gy") + sizes[1] + dy, sizes[1])
    return (gx, gy)


def exchange(buffer, sizes, columns, send_sem, recv_sem):
    copies = []
    for slot, (dx, dy) in enumerate(directions()):
        first, count, landing = 1, columns, 1
        if dy == 1:
            first, count, landing = columns, 1, 0
        if dy == -1:
            first, count, landing = 1, 1, columns + 1
        copies.append(
            pltpu.make_async_remote_copy(
                src_ref=buffer.at[1, pl.ds(first, count)],
                dst_ref=buffer.at[1 - dx, pl.ds(landing, count)],
                send_sem=send_sem.at[slot],
                recv_sem=recv_sem.at[slot],
                device_id=neighbour(sizes, dx, dy),
                device_id_type=MESH,
            )
        )
    for copy in copies:
        copy.start()
    return copies


def kernel(
    sizes, columns, depth, slots,
    pos_in, vel_in, mask_in, pos_out, vel_out, force_out,
    places, slopes, frame, near_rows, near_cols, self_rows, self_cols,
    own_slopes, held, totals, partial,
    place_send, place_recv, slope_send, slope_recv,
):
    wide = columns + 2
    f32, bf16 = jnp.float32, jnp.bfloat16
    cells = columns * depth

    barrier = pltpu.get_barrier_semaphore()
    greeted = [(dx, dy) for dx, dy in directions() if not (sizes[1] == 2 and dy == -1)]
    for dx, dy in greeted:
        pl.semaphore_signal(barrier, inc=1, device_id=neighbour(sizes, dx, dy), device_id_type=MESH)
    pl.semaphore_wait(barrier, len(greeted))

    for component in range(3):
        for column in range(columns):
            places[1, 1 + column, component] = pos_in[component, column]
            vel_out[component, column] = vel_in[component, column]
    for column in range(columns):
        places[1, 1 + column, 3] = mask_in[column]

    near_rows[...] = jnp.zeros_like(near_rows)
    self_rows[...] = jnp.zeros_like(self_rows)
    frame[...] = jnp.zeros_like(frame)
    ones = jnp.ones((depth, slots), f32)

    def put(ref, index, row, stride, value):
        ref[index + (pl.ds(row, depth, stride=stride), slice(None))] = value

    for v in range(wide):
        for u in range(3):
            for row in (21, 22, 23):
                put(near_rows, (u, v), row, FEATURES, ones)
    for column in range(columns):
        for r in range(3):
            for row in (18, 19, 20):
                put(self_rows, (r, column), row, FEATURES, ones)

    def build_column(u, v):
        mask = places[u, v, 3]
        spots = (
            places[u, v, 0] + (u - 1.5),
            places[u, v, 1] + (v - 1.0 - 0.5 * columns),
            places[u, v, 2] - 0.5,
        )
        norm = jnp.where(mask > 0.0, spots[0] * spots[0] + spots[1] * spots[1] + spots[2] * spots[2], ABSENT)
        for c in range(3):
            h, m, l = split3(spots[c])
            for place, value in enumerate((h, h, m, h, l, m)):
                put(near_rows, (u, v), 6 * c + place, FEATURES, value)
        for place, value in enumerate(split3(-norm)):
            put(near_rows, (u, v), 18 + place, FEATURES, value)
        for row, value in enumerate((spots[0], spots[1], spots[2] - 1.0, spots[2], spots[2] + 1.0)):
            put(frame, (u, v), row, 8, value)
        near_cols[v, :, u * slots:(u + 1) * slots] = near_rows[u, v].astype(bf16)

    def build_own(column):
        v = column + 1
        spots = (
            places[1, v, 0] - 0.5,
            places[1, v, 1] + (v - 1.0 - 0.5 * columns),
            places[1, v, 2] - 0.5,
        )
        for r in range(3):
            moved = (spots[0], spots[1], spots[2] - (r - 1.0))
            norm = moved[0] * moved[0] + moved[1] * moved[1] + moved[2] * moved[2]
            for c in range(3):
                h, m, l = split3(2.0 * moved[c])
                for place, value in enumerate((h, m, h, l, h, m)):
                    put(self_rows, (r, column), 6 * c + place, FEATURES, value)
            for place, value in enumerate(split3(1.0 - norm)):
                put(self_rows, (r, column), 21 + place, FEATURES, value)

    def turned(cell, carry):
        column, z = lax.div(cell, depth), lax.rem(cell, depth)
        rows = pl.ds(pl.multiple_of(z * FEATURES, FEATURES), FEATURES)
        for r in range(3):
            self_cols[r, cell] = self_rows[r, column, rows, :].T.astype(bf16)
        return carry

    def layers_of(z):
        return [lax.rem(z + r + depth, depth) for r in NEAR]

    def first_pass(cell, carry):
        column, z = lax.div(cell, depth), lax.rem(cell, depth)
        layers = layers_of(z)
        density = jnp.zeros((slots, slots), f32)
        for r in range(3):
            start = pl.multiple_of(layers[r] * FEATURES, FEATURES)
            for q in range(3):
                near = near_cols[column + q, pl.ds(start, FEATURES), :]
                reach = jnp.maximum(jnp.dot(self_cols[r, cell], near, preferred_element_type=f32), 0.0)
                for u in range(3):
                    part = reach[:, u * slots:(u + 1) * slots]
                    held[cell, (q * 3 + r) * 3 + u] = part
                    density = density + part * part
        present = places[1, column + 1, 3, pl.ds(z, 1), :]
        density = DENSITY_SCALE * (jnp.sum(density.T, axis=0, keepdims=True) - present)
        slope = DENSITY_SCALE / (4.0 * PAIR_SCALE) / jnp.sqrt(1.0 + density)
        slopes[1, column + 1, pl.ds(z, 1), :] = slope
        own_slopes[cell] = jnp.broadcast_to(slope, (slots, slots)).T
        return carry

    def second_pass(cell, carry):
        column, z = lax.div(cell, depth), lax.rem(cell, depth)
        layers = layers_of(z)
        for block in range(slots // TALL):
            rows = pl.ds(block * TALL, TALL)
            own = own_slopes[cell, rows, :]
            sums = [jnp.zeros((TALL, slots), f32)] * 4
            for q in range(3):
                for r in range(3):
                    for u in range(3):
                        at = [frame[u, column + q, pl.ds(layers[r] * 8 + row, 1), :] for row in (0, 1, 2 + r, 5)]
                        reach = held[cell, (q * 3 + r) * 3 + u, rows, :]
                        pull = reach * ((own + at[3]) - reach * reach)
                        for c in range(3):
                            sums[c] = sums[c] + pull * at[c]
                        sums[3] = sums[3] + pull
            for c in range(4):
                totals[c, rows, :] = sums[c]
        summed = [jnp.sum(totals[c].T, axis=0, keepdims=True) for c in range(4)]
        for c, row in enumerate((0, 1, 3)):
            own = frame[1, column + 1, pl.ds(z * 8 + row, 1), :]
            partial[column, pl.ds(z * 8 + c, 1), :] = (8.0 * PAIR_SCALE) * (summed[c] - own * summed[3])
        return carry

    def evaluate(step, carry):
        copies = exchange(places, sizes, columns, place_send, place_recv)
        for column in range(columns):
            build_own(column)
            build_column(1, column + 1)
        lax.fori_loop(0, cells, turned, 0)
        for copy in copies:
            copy.wait()
        for u in range(3):
            for v in range(wide):
                if u != 1 or v in (0, wide - 1):
                    build_column(u, v)
        lax.fori_loop(0, cells, first_pass, 0)
        copies = exchange(slopes, sizes, columns, slope_send, slope_recv)
        for copy in copies:
            copy.wait()
        for u in range(3):
            for v in range(wide):
                put(frame, (u, v), 5, 8, slopes[u, v])
        lax.fori_loop(0, cells, second_pass, 0)
        begin = jnp.where(step > 0, 0.5 * TIME_STEP, 0.0)
        end = jnp.where(step < STEPS, 0.5 * TIME_STEP, 0.0)
        drift = jnp.where(step < STEPS, TIME_STEP, 0.0)
        for column in range(columns):
            for c in range(3):
                force = partial[column, pl.ds(c, depth, stride=8), :] * places[1, column + 1, 3]
                force_out[c, column] = force
                speed = (vel_out[c, column] + begin * force) + end * force
                vel_out[c, column] = speed
                places[1, column + 1, c] = places[1, column + 1, c] + drift * speed
        return carry

    lax.fori_loop(0, STEPS + 1, evaluate, 0)
    for c in range(3):
        for column in range(columns):
            pos_out[c, column] = places[1, column + 1, c]


def shards(sizes, positions, velocities, counts):
    _, _, columns, depth, slots = positions.shape
    filled = lax.broadcasted_iota(jnp.int32, (columns, depth, slots), 2) < counts.reshape(columns, depth, 1)
    shape = (3, columns, depth, slots)
    wide = columns + 2
    cells = columns * depth
    f32, bf16 = jnp.float32, jnp.bfloat16
    vmem = pl.BlockSpec(memory_space=pltpu.VMEM)
    outs = pl.pallas_call(
        functools.partial(kernel, sizes, columns, depth, slots),
        out_shape=[jax.ShapeDtypeStruct(shape, f32)] * 3,
        in_specs=[vmem] * 3,
        out_specs=[vmem] * 3,
        scratch_shapes=[
            pltpu.VMEM((3, wide, 4, depth, slots), f32),
            pltpu.VMEM((3, wide, depth, slots), f32),
            pltpu.VMEM((3, wide, depth * 8, slots), f32),
            pltpu.VMEM((3, wide, depth * FEATURES, slots), f32),
            pltpu.VMEM((wide, depth * FEATURES, 3 * slots), bf16),
            pltpu.VMEM((3, columns, depth * FEATURES, slots), f32),
            pltpu.VMEM((3, cells, slots, FEATURES), bf16),
            pltpu.VMEM((cells, slots, slots), f32),
            pltpu.VMEM((cells, 27, slots, slots), f32),
            pltpu.VMEM((4, slots, slots), f32),
            pltpu.VMEM((columns, depth * 8, slots), f32),
            pltpu.SemaphoreType.DMA((8,)),
            pltpu.SemaphoreType.DMA((8,)),
            pltpu.SemaphoreType.DMA((8,)),
            pltpu.SemaphoreType.DMA((8,)),
        ],
        compiler_params=pltpu.CompilerParams(
            collective_id=0, has_side_effects=True, vmem_limit_bytes=60 * 1024 * 1024
        ),
        name="verlet",
    )(positions.reshape(shape), velocities.reshape(shape), filled.astype(f32))
    return tuple(out.reshape(positions.shape) for out in outs)


def solution(mesh):
    grid = P(None, "gx", "gy", None, None)
    sizes = (mesh.shape["gx"], mesh.shape["gy"])
    return jax.shard_map(
        functools.partial(shards, sizes),
        mesh=mesh,
        in_specs=(grid, grid, P("gx", "gy", None)),
        out_specs=(grid, grid, grid),
        check_vma=False,
    )
```

```python
import functools

import jax
import jax.numpy as jnp
from jax import lax
from jax.experimental import pallas as pl
from jax.experimental.pallas import tpu as pltpu
from jax.sharding import PartitionSpec as P

STEPS = 2
TIME_STEP = 0.05
DENSITY_SCALE = 0.0625
PAIR_SCALE = 0.0625
ABSENT = 1.0e6

FEATURES = 32
TALL = 32
LANES = (0, 2, 1)
NEAR = (-1, 0, 1)
MESH = pl.DeviceIdType.MESH


def split3(value):
    high = value.astype(jnp.bfloat16).astype(jnp.float32)
    rest = value - high
    middle = rest.astype(jnp.bfloat16).astype(jnp.float32)
    return high, middle, rest - middle


def directions():
    return [(dx, dy) for dx in NEAR for dy in NEAR if (dx, dy) != (0, 0)]


def neighbour(sizes, dx, dy):
    gx = lax.rem(lax.axis_index("gx") + sizes[0] + dx, sizes[0])
    gy = lax.rem(lax.axis_index("gy") + sizes[1] + dy, sizes[1])
    return (gx, gy)


def exchange(buffer, sizes, columns, send_sem, recv_sem):
    copies = []
    for slot, (dx, dy) in enumerate(directions()):
        first, count, landing = 1, columns, 1
        if dy == 1:
            first, count, landing = columns, 1, 0
        if dy == -1:
            first, count, landing = 1, 1, columns + 1
        copies.append(
            pltpu.make_async_remote_copy(
                src_ref=buffer.at[1, pl.ds(first, count)],
                dst_ref=buffer.at[1 - dx, pl.ds(landing, count)],
                send_sem=send_sem.at[slot],
                recv_sem=recv_sem.at[slot],
                device_id=neighbour(sizes, dx, dy),
                device_id_type=MESH,
            )
        )
    for copy in copies:
        copy.start()
    return copies


def kernel(
    sizes, columns, depth, slots,
    pos_in, vel_in, mask_in, pos_out, vel_out, force_out,
    places, slopes, frame, near_rows, near_cols, self_rows, self_cols,
    own_slopes, held, totals, partial,
    place_send, place_recv, slope_send, slope_recv,
):
    wide = columns + 2
    f32, bf16 = jnp.float32, jnp.bfloat16
    cells = columns * depth

    barrier = pltpu.get_barrier_semaphore()
    greeted = [(dx, dy) for dx, dy in directions() if not (sizes[1] == 2 and dy == -1)]
    for dx, dy in greeted:
        pl.semaphore_signal(barrier, inc=1, device_id=neighbour(sizes, dx, dy), device_id_type=MESH)
    pl.semaphore_wait(barrier, len(greeted))

    for component in range(3):
        for column in range(columns):
            places[1, 1 + column, component] = pos_in[component, column]
            vel_out[component, column] = vel_in[component, column]
    for column in range(columns):
        places[1, 1 + column, 3] = mask_in[column]

    near_rows[...] = jnp.zeros_like(near_rows)
    self_rows[...] = jnp.zeros_like(self_rows)
    frame[...] = jnp.zeros_like(frame)
    ones = jnp.ones((depth, slots), f32)

    def put(ref, index, row, stride, value):
        ref[index + (pl.ds(row, depth, stride=stride), slice(None))] = value

    for v in range(wide):
        for u in range(3):
            for row in (21, 22, 23):
                put(near_rows, (u, v), row, FEATURES, ones)
    for column in range(columns):
        for r in range(3):
            for row in (18, 19, 20):
                put(self_rows, (r, column), row, FEATURES, ones)

    def build_column(u, v):
        mask = places[u, v, 3]
        spots = (
            places[u, v, 0] + (u - 1.5),
            places[u, v, 1] + (v - 1.0 - 0.5 * columns),
            places[u, v, 2] - 0.5,
        )
        norm = jnp.where(mask > 0.0, spots[0] * spots[0] + spots[1] * spots[1] + spots[2] * spots[2], ABSENT)
        for c in range(3):
            h, m, l = split3(spots[c])
            for place, value in enumerate((h, h, m, h, l, m)):
                put(near_rows, (u, v), 6 * c + place, FEATURES, value)
        for place, value in enumerate(split3(-norm)):
            put(near_rows, (u, v), 18 + place, FEATURES, value)
        for row, value in enumerate((spots[0], spots[1], spots[2] - 1.0, spots[2], spots[2] + 1.0)):
            put(frame, (u, v), row, 8, value)
        near_cols[v, :, LANES[u] * slots:(LANES[u] + 1) * slots] = near_rows[u, v].astype(bf16)

    def build_own(column):
        v = column + 1
        spots = (
            places[1, v, 0] - 0.5,
            places[1, v, 1] + (v - 1.0 - 0.5 * columns),
            places[1, v, 2] - 0.5,
        )
        for r in range(3):
            moved = (spots[0], spots[1], spots[2] - (r - 1.0))
            norm = moved[0] * moved[0] + moved[1] * moved[1] + moved[2] * moved[2]
            for c in range(3):
                h, m, l = split3(2.0 * moved[c])
                for place, value in enumerate((h, m, h, l, h, m)):
                    put(self_rows, (r, column), 6 * c + place, FEATURES, value)
            for place, value in enumerate(split3(1.0 - norm)):
                put(self_rows, (r, column), 21 + place, FEATURES, value)

    def turned(cell, carry):
        column, z = lax.div(cell, depth), lax.rem(cell, depth)
        rows = pl.ds(pl.multiple_of(z * FEATURES, FEATURES), FEATURES)
        for r in range(3):
            self_cols[r, cell] = self_rows[r, column, rows, :].T.astype(bf16)
        return carry

    def layers_of(z):
        return [lax.rem(z + r + depth, depth) for r in NEAR]

    def own_side(column, q):
        return 1 <= column + q <= columns

    def reaches(cell, column, z, density, groups):
        layers = layers_of(z)
        for r in range(3):
            start = pl.multiple_of(layers[r] * FEATURES, FEATURES)
            for q, order in groups:
                low, high = LANES[order[0]], LANES[order[-1]] + 1
                near = near_cols[column + q, pl.ds(start, FEATURES), low * slots:high * slots]
                reach = jnp.maximum(jnp.dot(self_cols[r, cell], near, preferred_element_type=f32), 0.0)
                for place, u in enumerate(order):
                    part = reach[:, place * slots:(place + 1) * slots]
                    held[cell, (q * 3 + r) * 3 + u] = part
                    density = density + part * part
        return density

    def first_own(column, z, carry):
        cell = column * depth + z
        groups = [(q, (1,)) for q in range(3) if own_side(column, q)]
        own_slopes[cell] = reaches(cell, column, z, jnp.zeros((slots, slots), f32), groups)
        return carry

    def first_rest(column, z, carry):
        cell = column * depth + z
        groups = [(q, (0, 2) if own_side(column, q) else (0, 2, 1)) for q in range(3)]
        density = reaches(cell, column, z, own_slopes[cell], groups)
        present = places[1, column + 1, 3, pl.ds(z, 1), :]
        density = DENSITY_SCALE * (jnp.sum(density.T, axis=0, keepdims=True) - present)
        slope = DENSITY_SCALE / (4.0 * PAIR_SCALE) / jnp.sqrt(1.0 + density)
        slopes[1, column + 1, pl.ds(z, 1), :] = slope
        own_slopes[cell] = jnp.broadcast_to(slope, (slots, slots)).T
        return carry

    def pulls(cell, column, z, rows, sums, chosen):
        layers = layers_of(z)
        own = own_slopes[cell, rows, :]
        for q, u in chosen:
            for r in range(3):
                at = [frame[u, column + q, pl.ds(layers[r] * 8 + row, 1), :] for row in (0, 1, 2 + r, 5)]
                reach = held[cell, (q * 3 + r) * 3 + u, rows, :]
                pull = reach * ((own + at[3]) - reach * reach)
                for c in range(3):
                    sums[c] = sums[c] + pull * at[c]
                sums[3] = sums[3] + pull
        for c in range(4):
            totals[cell, c, rows, :] = sums[c]

    def second_own(column, z, carry):
        chosen = [(q, 1) for q in range(3) if own_side(column, q)]
        for block in range(slots // TALL):
            rows = pl.ds(block * TALL, TALL)
            pulls(column * depth + z, column, z, rows, [jnp.zeros((TALL, slots), f32)] * 4, chosen)
        return carry

    def second_rest(column, z, carry):
        cell = column * depth + z
        chosen = [(q, u) for q in range(3) for u in range(3) if u != 1 or not own_side(column, q)]
        for block in range(slots // TALL):
            rows = pl.ds(block * TALL, TALL)
            pulls(cell, column, z, rows, [totals[cell, c, rows, :] for c in range(4)], chosen)
        summed = [jnp.sum(totals[cell, c].T, axis=0, keepdims=True) for c in range(4)]
        for c, row in enumerate((0, 1, 3)):
            own = frame[1, column + 1, pl.ds(z * 8 + row, 1), :]
            partial[column, pl.ds(z * 8 + c, 1), :] = (8.0 * PAIR_SCALE) * (summed[c] - own * summed[3])
        return carry

    def over_cells(body):
        for column in range(columns):
            lax.fori_loop(0, depth, functools.partial(body, column), 0)

    halo = [(u, v) for u in range(3) for v in range(wide) if u != 1 or v in (0, wide - 1)]

    def evaluate(step, carry):
        copies = exchange(places, sizes, columns, place_send, place_recv)
        for column in range(columns):
            build_own(column)
            build_column(1, column + 1)
        lax.fori_loop(0, cells, turned, 0)
        over_cells(first_own)
        for copy in copies:
            copy.wait()
        for u, v in halo:
            build_column(u, v)
        over_cells(first_rest)
        copies = exchange(slopes, sizes, columns, slope_send, slope_recv)
        for v in range(1, columns + 1):
            put(frame, (1, v), 5, 8, slopes[1, v])
        over_cells(second_own)
        for copy in copies:
            copy.wait()
        for u, v in halo:
            put(frame, (u, v), 5, 8, slopes[u, v])
        over_cells(second_rest)
        begin = jnp.where(step > 0, 0.5 * TIME_STEP, 0.0)
        end = jnp.where(step < STEPS, 0.5 * TIME_STEP, 0.0)
        drift = jnp.where(step < STEPS, TIME_STEP, 0.0)
        for column in range(columns):
            for c in range(3):
                force = partial[column, pl.ds(c, depth, stride=8), :] * places[1, column + 1, 3]
                force_out[c, column] = force
                speed = (vel_out[c, column] + begin * force) + end * force
                vel_out[c, column] = speed
                places[1, column + 1, c] = places[1, column + 1, c] + drift * speed
        return carry

    lax.fori_loop(0, STEPS + 1, evaluate, 0)
    for c in range(3):
        for column in range(columns):
            pos_out[c, column] = places[1, column + 1, c]


def shards(sizes, positions, velocities, counts):
    _, _, columns, depth, slots = positions.shape
    filled = lax.broadcasted_iota(jnp.int32, (columns, depth, slots), 2) < counts.reshape(columns, depth, 1)
    shape = (3, columns, depth, slots)
    wide = columns + 2
    cells = columns * depth
    f32, bf16 = jnp.float32, jnp.bfloat16
    vmem = pl.BlockSpec(memory_space=pltpu.VMEM)
    outs = pl.pallas_call(
        functools.partial(kernel, sizes, columns, depth, slots),
        out_shape=[jax.ShapeDtypeStruct(shape, f32)] * 3,
        in_specs=[vmem] * 3,
        out_specs=[vmem] * 3,
        scratch_shapes=[
            pltpu.VMEM((3, wide, 4, depth, slots), f32),
            pltpu.VMEM((3, wide, depth, slots), f32),
            pltpu.VMEM((3, wide, depth * 8, slots), f32),
            pltpu.VMEM((3, wide, depth * FEATURES, slots), f32),
            pltpu.VMEM((wide, depth * FEATURES, 3 * slots), bf16),
            pltpu.VMEM((3, columns, depth * FEATURES, slots), f32),
            pltpu.VMEM((3, cells, slots, FEATURES), bf16),
            pltpu.VMEM((cells, slots, slots), f32),
            pltpu.VMEM((cells, 27, slots, slots), f32),
            pltpu.VMEM((cells, 4, slots, slots), f32),
            pltpu.VMEM((columns, depth * 8, slots), f32),
            pltpu.SemaphoreType.DMA((8,)),
            pltpu.SemaphoreType.DMA((8,)),
            pltpu.SemaphoreType.DMA((8,)),
            pltpu.SemaphoreType.DMA((8,)),
        ],
        compiler_params=pltpu.CompilerParams(
            collective_id=0, has_side_effects=True, vmem_limit_bytes=60 * 1024 * 1024
        ),
        name="verlet",
    )(positions.reshape(shape), velocities.reshape(shape), filled.astype(f32))
    return tuple(out.reshape(positions.shape) for out in outs)


def solution(mesh):
    grid = P(None, "gx", "gy", None, None)
    sizes = (mesh.shape["gx"], mesh.shape["gy"])
    return jax.shard_map(
        functools.partial(shards, sizes),
        mesh=mesh,
        in_specs=(grid, grid, P("gx", "gy", None)),
        out_specs=(grid, grid, grid),
        check_vma=False,
    )
```

```python
import functools

import jax
import jax.numpy as jnp
from jax import lax
from jax.experimental import pallas as pl
from jax.experimental.pallas import tpu as pltpu
from jax.sharding import PartitionSpec as P

STEPS = 2
TIME_STEP = 0.05
DENSITY_SCALE = 0.0625
PAIR_SCALE = 0.0625
ABSENT = 1.0e6

FEATURES = 32
TALL = 64
LANES = (0, 2, 1)
NEAR = (-1, 0, 1)
MESH = pl.DeviceIdType.MESH


def split3(value):
    high = value.astype(jnp.bfloat16).astype(jnp.float32)
    rest = value - high
    middle = rest.astype(jnp.bfloat16).astype(jnp.float32)
    return high, middle, rest - middle


def directions():
    return [(dx, dy) for dx in NEAR for dy in NEAR if (dx, dy) != (0, 0)]


def neighbour(sizes, dx, dy):
    gx = lax.rem(lax.axis_index("gx") + sizes[0] + dx, sizes[0])
    gy = lax.rem(lax.axis_index("gy") + sizes[1] + dy, sizes[1])
    return (gx, gy)


def exchange(buffer, sizes, columns, send_sem, recv_sem):
    copies = []
    for slot, (dx, dy) in enumerate(directions()):
        first, count, landing = 1, columns, 1
        if dy == 1:
            first, count, landing = columns, 1, 0
        if dy == -1:
            first, count, landing = 1, 1, columns + 1
        copies.append(
            pltpu.make_async_remote_copy(
                src_ref=buffer.at[1, pl.ds(first, count)],
                dst_ref=buffer.at[1 - dx, pl.ds(landing, count)],
                send_sem=send_sem.at[slot],
                recv_sem=recv_sem.at[slot],
                device_id=neighbour(sizes, dx, dy),
                device_id_type=MESH,
            )
        )
    for copy in copies:
        copy.start()
    return copies


def kernel(
    sizes, columns, depth, slots,
    pos_in, vel_in, mask_in, pos_out, vel_out, force_out,
    places, slopes, frame, near_rows, near_cols, self_rows, self_cols,
    own_slopes, held, totals, partial,
    place_send, place_recv, slope_send, slope_recv,
):
    wide = columns + 2
    f32, bf16 = jnp.float32, jnp.bfloat16
    cells = columns * depth

    barrier = pltpu.get_barrier_semaphore()
    greeted = [(dx, dy) for dx, dy in directions() if not (sizes[1] == 2 and dy == -1)]
    for dx, dy in greeted:
        pl.semaphore_signal(barrier, inc=1, device_id=neighbour(sizes, dx, dy), device_id_type=MESH)
    pl.semaphore_wait(barrier, len(greeted))

    for component in range(3):
        for column in range(columns):
            places[1, 1 + column, component] = pos_in[component, column]
            vel_out[component, column] = vel_in[component, column]
    for column in range(columns):
        places[1, 1 + column, 3] = mask_in[column]

    near_rows[...] = jnp.zeros_like(near_rows)
    self_rows[...] = jnp.zeros_like(self_rows)
    frame[...] = jnp.zeros_like(frame)
    ones = jnp.ones((depth, slots), f32)

    def put(ref, index, row, stride, value):
        ref[index + (pl.ds(row, depth, stride=stride), slice(None))] = value

    for v in range(wide):
        for u in range(3):
            for row in (21, 22, 23):
                put(near_rows, (u, v), row, FEATURES, ones)
    for column in range(columns):
        for r in range(3):
            for row in (18, 19, 20):
                put(self_rows, (r, column), row, FEATURES, ones)

    def build_column(u, v):
        mask = places[u, v, 3]
        spots = (
            places[u, v, 0] + (u - 1.5),
            places[u, v, 1] + (v - 1.0 - 0.5 * columns),
            places[u, v, 2] - 0.5,
        )
        norm = jnp.where(mask > 0.0, spots[0] * spots[0] + spots[1] * spots[1] + spots[2] * spots[2], ABSENT)
        for c in range(3):
            h, m, l = split3(spots[c])
            for place, value in enumerate((h, h, m, h, l, m)):
                put(near_rows, (u, v), 6 * c + place, FEATURES, value)
        for place, value in enumerate(split3(-norm)):
            put(near_rows, (u, v), 18 + place, FEATURES, value)
        for row, value in enumerate((spots[0], spots[1], spots[2] - 1.0, spots[2], spots[2] + 1.0)):
            put(frame, (u, v), row, 8, value)
        near_cols[v, :, LANES[u] * slots:(LANES[u] + 1) * slots] = near_rows[u, v].astype(bf16)

    def build_own(column):
        v = column + 1
        spots = (
            places[1, v, 0] - 0.5,
            places[1, v, 1] + (v - 1.0 - 0.5 * columns),
            places[1, v, 2] - 0.5,
        )
        for r in range(3):
            moved = (spots[0], spots[1], spots[2] - (r - 1.0))
            norm = moved[0] * moved[0] + moved[1] * moved[1] + moved[2] * moved[2]
            for c in range(3):
                h, m, l = split3(2.0 * moved[c])
                for place, value in enumerate((h, m, h, l, h, m)):
                    put(self_rows, (r, column), 6 * c + place, FEATURES, value)
            for place, value in enumerate(split3(1.0 - norm)):
                put(self_rows, (r, column), 21 + place, FEATURES, value)

    def turned(cell, carry):
        column, z = lax.div(cell, depth), lax.rem(cell, depth)
        rows = pl.ds(pl.multiple_of(z * FEATURES, FEATURES), FEATURES)
        for r in range(3):
            self_cols[r, cell] = self_rows[r, column, rows, :].T.astype(bf16)
        return carry

    def layers_of(z):
        return [lax.rem(z + r + depth, depth) for r in NEAR]

    def own_side(column, q):
        return 1 <= column + q <= columns

    def reaches(cell, column, z, density, groups):
        layers = layers_of(z)
        for r in range(3):
            start = pl.multiple_of(layers[r] * FEATURES, FEATURES)
            for q, order in groups:
                low, high = LANES[order[0]], LANES[order[-1]] + 1
                near = near_cols[column + q, pl.ds(start, FEATURES), low * slots:high * slots]
                reach = jnp.maximum(jnp.dot(self_cols[r, cell], near, preferred_element_type=f32), 0.0)
                for place, u in enumerate(order):
                    part = reach[:, place * slots:(place + 1) * slots]
                    held[cell, (q * 3 + r) * 3 + u] = part
                    density = density + part * part
        return density

    def first_own(column, z, carry):
        cell = column * depth + z
        groups = [(q, (1,)) for q in range(3) if own_side(column, q)]
        own_slopes[cell] = reaches(cell, column, z, jnp.zeros((slots, slots), f32), groups)
        return carry

    def first_rest(column, z, carry):
        cell = column * depth + z
        groups = [(q, (0, 2) if own_side(column, q) else (0, 2, 1)) for q in range(3)]
        density = reaches(cell, column, z, own_slopes[cell], groups)
        present = places[1, column + 1, 3, pl.ds(z, 1), :]
        density = DENSITY_SCALE * (jnp.sum(density.T, axis=0, keepdims=True) - present)
        slope = DENSITY_SCALE / (4.0 * PAIR_SCALE) / jnp.sqrt(1.0 + density)
        slopes[1, column + 1, pl.ds(z, 1), :] = slope
        own_slopes[cell] = jnp.broadcast_to(slope, (slots, slots)).T
        return carry

    def pulls(cell, column, z, rows, sums, chosen):
        layers = layers_of(z)
        own = own_slopes[cell, rows, :]
        for q, u in chosen:
            for r in range(3):
                at = [frame[u, column + q, pl.ds(layers[r] * 8 + row, 1), :] for row in (0, 1, 2 + r, 5)]
                reach = held[cell, (q * 3 + r) * 3 + u, rows, :]
                pull = reach * ((own + at[3]) - reach * reach)
                for c in range(3):
                    sums[c] = sums[c] + pull * at[c]
                sums[3] = sums[3] + pull
        for c in range(4):
            totals[cell, c, rows, :] = sums[c]

    def second_own(column, z, carry):
        chosen = [(q, 1) for q in range(3) if own_side(column, q)]
        for block in range(slots // TALL):
            rows = pl.ds(block * TALL, TALL)
            pulls(column * depth + z, column, z, rows, [jnp.zeros((TALL, slots), f32)] * 4, chosen)
        return carry

    def second_rest(column, z, carry):
        cell = column * depth + z
        chosen = [(q, u) for q in range(3) for u in range(3) if u != 1 or not own_side(column, q)]
        for block in range(slots // TALL):
            rows = pl.ds(block * TALL, TALL)
            pulls(cell, column, z, rows, [totals[cell, c, rows, :] for c in range(4)], chosen)
        summed = [jnp.sum(totals[cell, c].T, axis=0, keepdims=True) for c in range(4)]
        for c, row in enumerate((0, 1, 3)):
            own = frame[1, column + 1, pl.ds(z * 8 + row, 1), :]
            partial[column, pl.ds(z * 8 + c, 1), :] = (8.0 * PAIR_SCALE) * (summed[c] - own * summed[3])
        return carry

    def over_cells(body):
        for column in range(columns):
            lax.fori_loop(0, depth, functools.partial(body, column), 0)

    halo = [(u, v) for u in range(3) for v in range(wide) if u != 1 or v in (0, wide - 1)]

    def evaluate(step, carry):
        copies = exchange(places, sizes, columns, place_send, place_recv)
        for column in range(columns):
            build_own(column)
            build_column(1, column + 1)
        lax.fori_loop(0, cells, turned, 0)
        over_cells(first_own)
        for copy in copies:
            copy.wait()
        for u, v in halo:
            build_column(u, v)
        over_cells(first_rest)
        copies = exchange(slopes, sizes, columns, slope_send, slope_recv)
        for v in range(1, columns + 1):
            put(frame, (1, v), 5, 8, slopes[1, v])
        over_cells(second_own)
        for copy in copies:
            copy.wait()
        for u, v in halo:
            put(frame, (u, v), 5, 8, slopes[u, v])
        over_cells(second_rest)
        begin = jnp.where(step > 0, 0.5 * TIME_STEP, 0.0)
        end = jnp.where(step < STEPS, 0.5 * TIME_STEP, 0.0)
        drift = jnp.where(step < STEPS, TIME_STEP, 0.0)
        for column in range(columns):
            for c in range(3):
                force = partial[column, pl.ds(c, depth, stride=8), :] * places[1, column + 1, 3]
                force_out[c, column] = force
                speed = (vel_out[c, column] + begin * force) + end * force
                vel_out[c, column] = speed
                places[1, column + 1, c] = places[1, column + 1, c] + drift * speed
        return carry

    lax.fori_loop(0, STEPS + 1, evaluate, 0)
    for c in range(3):
        for column in range(columns):
            pos_out[c, column] = places[1, column + 1, c]


def shards(sizes, positions, velocities, counts):
    _, _, columns, depth, slots = positions.shape
    filled = lax.broadcasted_iota(jnp.int32, (columns, depth, slots), 2) < counts.reshape(columns, depth, 1)
    shape = (3, columns, depth, slots)
    wide = columns + 2
    cells = columns * depth
    f32, bf16 = jnp.float32, jnp.bfloat16
    vmem = pl.BlockSpec(memory_space=pltpu.VMEM)
    outs = pl.pallas_call(
        functools.partial(kernel, sizes, columns, depth, slots),
        out_shape=[jax.ShapeDtypeStruct(shape, f32)] * 3,
        in_specs=[vmem] * 3,
        out_specs=[vmem] * 3,
        scratch_shapes=[
            pltpu.VMEM((3, wide, 4, depth, slots), f32),
            pltpu.VMEM((3, wide, depth, slots), f32),
            pltpu.VMEM((3, wide, depth * 8, slots), f32),
            pltpu.VMEM((3, wide, depth * FEATURES, slots), f32),
            pltpu.VMEM((wide, depth * FEATURES, 3 * slots), bf16),
            pltpu.VMEM((3, columns, depth * FEATURES, slots), f32),
            pltpu.VMEM((3, cells, slots, FEATURES), bf16),
            pltpu.VMEM((cells, slots, slots), f32),
            pltpu.VMEM((cells, 27, slots, slots), f32),
            pltpu.VMEM((cells, 4, slots, slots), f32),
            pltpu.VMEM((columns, depth * 8, slots), f32),
            pltpu.SemaphoreType.DMA((8,)),
            pltpu.SemaphoreType.DMA((8,)),
            pltpu.SemaphoreType.DMA((8,)),
            pltpu.SemaphoreType.DMA((8,)),
        ],
        compiler_params=pltpu.CompilerParams(
            collective_id=0, has_side_effects=True, vmem_limit_bytes=60 * 1024 * 1024
        ),
        name="verlet",
    )(positions.reshape(shape), velocities.reshape(shape), filled.astype(f32))
    return tuple(out.reshape(positions.shape) for out in outs)


def solution(mesh):
    grid = P(None, "gx", "gy", None, None)
    sizes = (mesh.shape["gx"], mesh.shape["gy"])
    return jax.shard_map(
        functools.partial(shards, sizes),
        mesh=mesh,
        in_specs=(grid, grid, P("gx", "gy", None)),
        out_specs=(grid, grid, grid),
        check_vma=False,
    )
```
